512 devices in a mesh: dp: 64 (over z, x, y_hi), tensor: 8 (over y_lo, core).
Axes of the slice: x: 4, y: 8 (y_hi: 2, y_lo: 4; y = y_hi * 4 + y_lo), z: 8, core: 2. Of those that a mesh axis runs over, the one named last changes fastest.
Arguments:
- activations: bfloat16 [65536, 8192], P(('dp', 'tensor')), may hold values from -64 to 64
- out_grads: bfloat16 [65536, 10240], P('dp', 'tensor'), may hold values from -64 to 64
- act_old: float32 [16, 512, 512], P('tensor', 'dp'), may hold values from -20 to 44, as said below
- grad_old: float32 [40, 256, 256], P('tensor', 'dp'), may hold values from -20 to 44, as said below
Outputs:
- act_new: float32 [16, 512, 512], P('tensor', 'dp')
- grad_new: float32 [40, 256, 256], P('tensor', 'dp')
The draws below stay inside these ranges and needn't reach their ends.
Inputs may be any that keep to these rules, and one draw needn't show every extreme that they name: `act_old`: each block is symmetric. `grad_old`: each block is symmetric.
All inputs are finite; a program needn't handle non-finite values.
Results may differ from the reference program's by a relative error of at most 0.0003.
Values may be sent and summed in bfloat16 or wider, within the bound.
A program may use at most 64 MiB of HBM per device.

```python
import jax
import jax.numpy as jnp
from jax import lax

ABLK = 512
GBLK = 256
TOKENS = 65536
NABLK = 16
NGBLK = 40


mix_weight = 0.6


def mixed_columns(key, total_rows, width, block_count):
    key_rows, key_blocks = jax.random.split(key)
    row_scale = jnp.exp(jax.random.uniform(key_rows, (total_rows, 1), jnp.float32, jnp.log(0.3), jnp.log(3.0)))

    def one_block(block_index):
        block_key = jax.random.fold_in(key_blocks, block_index)
        key_noise = jax.random.fold_in(block_key, 0)
        key_cols = jax.random.fold_in(block_key, 1)
        key_mix = jax.random.fold_in(block_key, 3)
        col_scale = jnp.exp(jax.random.uniform(key_cols, (1, width), jnp.float32, jnp.log(0.5), jnp.log(2.0)))
        noise = jnp.clip(jax.random.normal(key_noise, (total_rows, width), jnp.float32), -6.0, 6.0)
        mixed = noise
        for turn in range(4):
            key_perm, key_sign = jax.random.split(jax.random.fold_in(key_mix, turn))
            order = jax.random.permutation(key_perm, jnp.arange(width, dtype=jnp.int32))
            signs = (2 * jax.random.randint(key_sign, (width,), 0, 2) - 1).astype(jnp.float32)
            mixed = mixed + mix_weight * signs[None, :] * jnp.take(noise, order, axis=1)
        mixed = jnp.clip(mixed, -10.0, 10.0)
        return (mixed * col_scale * row_scale).astype(jnp.bfloat16)
    blocks = lax.map(one_block, jnp.arange(block_count, dtype=jnp.int32))
    return jnp.transpose(blocks, (1, 0, 2)).reshape(total_rows, block_count * width)


def factor_blocks(key, block_count, width):
    key_scale, key_diag, key_low = jax.random.split(key, 3)
    scale = jnp.exp(jax.random.uniform(key_scale, (block_count, width), jnp.float32, jnp.log(0.5), jnp.log(2.0)))
    diag = jax.random.uniform(key_diag, (block_count, width), jnp.float32, 2.0, 6.0)
    low = jnp.clip(jax.random.normal(key_low, (block_count, width), jnp.float32), -3.0, 3.0)
    index = jnp.arange(width, dtype=jnp.int32)
    ident = (index[:, None] == index[None, :]).astype(jnp.float32)
    inner = ident[None, :, :] * diag[:, :, None] + 0.5 * low[:, :, None] * low[:, None, :]
    return scale[:, :, None] * scale[:, None, :] * inner


def draw_activations(key, part):
    key = jax.random.fold_in(key, 11)
    return mixed_columns(key, TOKENS, ABLK, NABLK)


def draw_out_grads(key, part):
    key = jax.random.fold_in(key, 23)
    return mixed_columns(key, TOKENS, GBLK, NGBLK)


def draw_act_old(key, part):
    key = jax.random.fold_in(key, 37)
    return factor_blocks(key, NABLK, ABLK)


def draw_grad_old(key, part):
    key = jax.random.fold_in(key, 41)
    return factor_blocks(key, NGBLK, GBLK)


def setup_inputs(seed: int = 0) -> dict:
    streams_of = jax.random.split(jax.random.key(seed), 5)
    activations = draw_activations(jax.random.fold_in(streams_of[4], 71), 0)
    out_grads = draw_out_grads(jax.random.fold_in(streams_of[4], 71), 0)
    act_old = draw_act_old(jax.random.fold_in(streams_of[4], 71), 0)
    grad_old = draw_grad_old(jax.random.fold_in(streams_of[4], 71), 0)
    return {"activations": activations, "out_grads": out_grads, "act_old": act_old, "grad_old": grad_old}


DECAY_RATE = 0.5


def block_cov(matrix, block_width, block_count):
    def one_block(block_index):
        piece = lax.dynamic_slice_in_dim(matrix, block_index * block_width, block_width, 1)
        return jnp.dot(piece.T, piece, preferred_element_type=jnp.float32)
    return lax.map(one_block, jnp.arange(block_count, dtype=jnp.int32))


def reference(activations, out_grads, act_old, grad_old):
    norm_scale = (1.0 - DECAY_RATE) / TOKENS
    act_cov = block_cov(activations, ABLK, NABLK)
    grad_cov = block_cov(out_grads, GBLK, NGBLK)
    act_new = DECAY_RATE * act_old + norm_scale * act_cov
    grad_new = DECAY_RATE * grad_old + norm_scale * grad_cov
    return act_new, grad_new
```

```python
import functools

import jax
import jax.numpy as jnp
from jax import lax
from jax.experimental import pallas as pl
from jax.experimental.pallas import tpu as pltpu
from jax.sharding import PartitionSpec as P

MESH = pl.DeviceIdType.MESH
F32 = jnp.float32
BF16 = jnp.bfloat16
DECAY_RATE = 0.5

FIRST = BF16
X, Y, Z = 0, 1, 2
ORDERS = ((X, Y, Z), (X, Z, Y), (Y, X, Z), (Z, X, Y))


def gram(left, right):
    return lax.dot_general(left, right, (((0,), (0,)), ((), ())), preferred_element_type=F32)


def kernel(
    act_ref, grad_ref, act_out, grad_out,
    gv, xo, xc, xy, xz, xd, acc,
    a_own, a_snd, a_r1, a_s2, a_r2, a_s3, a_r3, fin, fin_r,
    g_own, g_snd, g_r1, g_s2, g_r2, g_s3, g_r3,
    local_sem, tok_send, tok_recv, a_send, a_recv, fin_sem, g_send, g_recv,
):
    dp = lax.axis_index("dp")
    tensor = lax.axis_index("tensor")
    yh = dp % 2
    x = (dp // 2) % 4
    z = dp // 8
    c = tensor % 2
    y = yh * 4 + tensor // 2
    yp, zp = y % 2, z % 2
    q, m = y // 2, z // 2

    def device(zz, xx, yy, cc):
        return ((zz * 4 + xx) * 2 + yy // 4, (yy % 4) * 2 + cc)

    def columns(half, ypar, core, zpar):
        return pl.ds(pl.multiple_of((half * 8 + ypar * 4 + core * 2 + zpar) * 512, 512), 512)

    def send(src, dst, send_sem, recv_sem, target):
        pltpu.make_async_remote_copy(
            src_ref=src, dst_ref=dst, send_sem=send_sem, recv_sem=recv_sem,
            device_id=target, device_id_type=MESH,
        ).start()

    here = (dp, tensor)

    def arrived(buf, sem):
        pltpu.make_async_remote_copy(
            src_ref=buf, dst_ref=buf, send_sem=sem, recv_sem=sem,
            device_id=here, device_id_type=MESH,
        ).wait_recv()

    def left(buf, sem):
        pltpu.make_async_remote_copy(
            src_ref=buf, dst_ref=buf, send_sem=sem, recv_sem=sem,
            device_id=here, device_id_type=MESH,
        ).wait_send()

    grads_in = pltpu.make_async_copy(grad_ref, gv, local_sem.at[0])
    grads_in.start()
    own_in = [
        pltpu.make_async_copy(act_ref.at[:, columns(h, yp, c, zp)], xo.at[h], local_sem.at[1 + h])
        for h in range(2)
    ]
    for copy in own_in:
        copy.start()

    yn = ((y + 1) % 8, (y + 7) % 8)
    zn = ((z + 1) % 8, (z + 7) % 8)
    cores = (c, 1 - c)
    oy, oz = 1 - yp, 1 - zp

    peers = [device(z, x, y, 1 - c)]
    peers += [device(z, x, yn[s], cores[f]) for s in range(2) for f in range(2)]
    peers += [device(zn[s], x, y, cores[f]) for s in range(2) for f in range(2)]
    peers += [device(zn[t], x, yn[s], cores[f]) for s in range(2) for t in range(2) for f in range(2)]
    peers += [device(z, (x + k) % 4, y, c) for k in range(1, 4)]
    peers += [device(z, x, (y + 2 * k) % 8, c) for k in range(1, 4)]
    peers += [device((z + k) % 8, x, y, c) for k in range(2, 7)]
    barrier = pltpu.get_barrier_semaphore()
    for peer in peers:
        pl.semaphore_signal(barrier, inc=1, device_id=peer, device_id_type=MESH)
    pl.semaphore_wait(barrier, len(peers))

    for s in range(2):
        for t in range(2):
            for f in range(2):
                n = s * 2 + t
                for h in range(2):
                    send(
                        act_ref.at[pl.ds(n * 32, 32), columns(h, oy, cores[f], oz)],
                        xd.at[h, pl.ds((n * 2 + f) * 32, 32)],
                        tok_send.at[3], tok_recv.at[3], device(zn[t], x, yn[s], cores[f]),
                    )
    for s in range(2):
        for f in range(2):
            for h in range(2):
                send(
                    act_ref.at[pl.ds(s * 64, 64), columns(h, oy, cores[f], zp)],
                    xy.at[h, pl.ds((s * 2 + f) * 64, 64)],
                    tok_send.at[1], tok_recv.at[1], device(z, x, yn[s], cores[f]),
                )
                send(
                    act_ref.at[pl.ds(s * 64, 64), columns(h, yp, cores[f], oz)],
                    xz.at[h, pl.ds((s * 2 + f) * 64, 64)],
                    tok_send.at[2], tok_recv.at[2], device(zn[s], x, y, cores[f]),
                )
    for h in range(2):
        send(
            act_ref.at[:, columns(h, yp, 1 - c, zp)], xc.at[h],
            tok_send.at[0], tok_recv.at[0], device(z, x, y, 1 - c),
        )

    grads_in.wait()
    for b in range(5):
        block = gv[:, b * 256:(b + 1) * 256]
        part = gram(block, block)
        for xx in range(4):
            for mm in range(4):
                r = mm * 64 + xx * 8
                rows = jnp.concatenate([part[r:r + 8], part[r + 32:r + 40]], axis=0)
                g_own[xx, mm, b] = rows
                g_snd[xx, mm, b] = rows.astype(FIRST)
    for k in range(1, 4):
        to = (x + k) % 4
        send(g_snd.at[to], g_r1.at[k - 1], g_send.at[0], g_recv.at[0], device(z, to, y, c))

    for copy in own_in:
        copy.wait()
    for h in range(2):
        for i in range(2):
            acc[h, i * 256:(i + 1) * 256] = gram(xo[h, :, i * 256:(i + 1) * 256], xo[h])
    for buf, g in ((xc, 0), (xy, 1), (xz, 2)):
        arrived(buf, tok_recv.at[g])
        for h in range(2):
            for i in range(2):
                acc[h, i * 256:(i + 1) * 256] += gram(buf[h, :, i * 256:(i + 1) * 256], buf[h])
    arrived(xd, tok_recv.at[3])
    for h in range(2):
        for mm in range(4):
            part = acc[h, mm * 128:(mm + 1) * 128] + gram(xd[h, :, mm * 128:(mm + 1) * 128], xd[h])
            for xx in range(4):
                for hi in range(2):
                    r = xx * 16 + hi * 8
                    rows = jnp.concatenate([part[r:r + 8], part[r + 64:r + 72]], axis=0)
                    at = (xx, hi * 2 + h, mm)
                    for p in range(4):
                        i1, i2, i3 = (at[axis] for axis in ORDERS[p])
                        piece = rows[:, p * 128:(p + 1) * 128]
                        a_own[p, i1, i2, i3] = piece
                        a_snd[p, i1, i2, i3] = piece.astype(FIRST)

    me = (x, q, m)

    def scatter(src, dst, axis, send_sem, recv_sem):
        for k in (2, 1, 3):
            to = (me[axis] + k) % 4
            target = (
                device(z, to, y, c) if axis == X
                else device(z, x, (y + 2 * k) % 8, c) if axis == Y
                else device((z + 2 * k) % 8, x, y, c)
            )
            send(src.at[to], dst.at[k - 1], send_sem, recv_sem, target)

    for p in (2, 3, 0, 1):
        scatter(a_snd.at[p], a_r1.at[p], ORDERS[p][0], a_send.at[p, 0], a_recv.at[p, 0])

    arrived(g_r1, g_recv.at[0])
    for mm in range(4):
        for b in range(5):
            rows = g_own[x, mm, b]
            for k in range(3):
                rows += g_r1[k, mm, b].astype(F32)
            g_s2[2 * mm, b] = rows[:8]
            g_s2[2 * mm + 1, b] = rows[8:]
    for k in (4, 3, 5, 2, 6, 1, 7):
        to = (z + k) % 8
        send(g_s2.at[to], g_r2.at[k - 1], g_send.at[1], g_recv.at[1], device(to, x, y, c))

    for p in range(4):
        arrived(a_r1.at[p], a_recv.at[p, 0])
        own = me[ORDERS[p][0]]
        total = a_own[p, own]
        for k in range(3):
            total += a_r1[p, k].astype(F32)
        a_s2[p] = total
        scatter(a_s2.at[p], a_r2.at[p], ORDERS[p][1], a_send.at[p, 1], a_recv.at[p, 1])

    arrived(g_r2, g_recv.at[1])
    rest = g_s2[z]
    for k in range(7):
        rest += g_r2[k]
    g_s3[...] = rest
    send(g_s3, g_r3, g_send.at[2], g_recv.at[2], device(z, x, (y + 4) % 8, c))

    for p in range(4):
        arrived(a_r2.at[p], a_recv.at[p, 1])
        own = me[ORDERS[p][1]]
        total = a_s2[p, own]
        for k in range(3):
            total += a_r2[p, k]
        a_s3[p] = total
        scatter(a_s3.at[p], a_r3.at[p], ORDERS[p][2], a_send.at[p, 2], a_recv.at[p, 2])

    for p in range(4):
        arrived(a_r3.at[p], a_recv.at[p, 2])
        own = me[ORDERS[p][2]]
        total = a_s3[p, own]
        for k in range(3):
            total += a_r3[p, k]
        fin[0, :, p * 128:(p + 1) * 128] = total[:8]
        fin[1, :, p * 128:(p + 1) * 128] = total[8:]
    partner = device(z + 1 - 2 * zp, x, y, c)
    send(fin.at[oz], fin_r, fin_sem.at[0], fin_sem.at[1], partner)
    arrived(g_r3, g_recv.at[2])
    grad_out[...] = g_s3[...] + g_r3[...]
    act_out[zp] = fin[zp]
    arrived(fin_r, fin_sem.at[1])
    act_out[oz] = fin_r[...]

    for buf, g in ((xc, 0), (xy, 1), (xz, 2), (xd, 3)):
        left(buf, tok_send.at[g])
    for p in range(4):
        left(a_r1.at[p], a_send.at[p, 0])
        left(a_r2.at[p], a_send.at[p, 1])
        left(a_r3.at[p], a_send.at[p, 2])
    left(g_r1, g_send.at[0])
    left(g_r2, g_send.at[1])
    left(g_r3, g_send.at[2])
    left(fin_r, fin_sem.at[0])


def statistics(activations, out_grads):
    any_spec = pl.BlockSpec(memory_space=pl.ANY)
    vmem_spec = pl.BlockSpec(memory_space=pltpu.VMEM)
    vmem = pltpu.VMEM
    dma = pltpu.SemaphoreType.DMA
    return pl.pallas_call(
        kernel,
        out_shape=(jax.ShapeDtypeStruct((2, 8, 512), F32), jax.ShapeDtypeStruct((5, 8, 256), F32)),
        in_specs=[any_spec, any_spec],
        out_specs=(vmem_spec, vmem_spec),
        scratch_shapes=[
            vmem((1024, 1280), BF16),
            vmem((2, 128, 512), BF16),
            vmem((2, 128, 512), BF16),
            vmem((2, 256, 512), BF16),
            vmem((2, 256, 512), BF16),
            vmem((2, 256, 512), BF16),
            vmem((2, 512, 512), F32),
            vmem((4, 4, 4, 4, 16, 128), F32),
            vmem((4, 4, 4, 4, 16, 128), FIRST),
            vmem((4, 3, 4, 4, 16, 128), FIRST),
            vmem((4, 4, 4, 16, 128), F32),
            vmem((4, 3, 4, 16, 128), F32),
            vmem((4, 4, 16, 128), F32),
            vmem((4, 3, 16, 128), F32),
            vmem((2, 8, 512), F32),
            vmem((8, 512), F32),
            vmem((4, 4, 5, 16, 256), F32),
            vmem((4, 4, 5, 16, 256), FIRST),
            vmem((3, 4, 5, 16, 256), FIRST),
            vmem((8, 5, 8, 256), F32),
            vmem((7, 5, 8, 256), F32),
            vmem((5, 8, 256), F32),
            vmem((5, 8, 256), F32),
            dma((3,)),
            dma((4,)),
            dma((4,)),
            dma((4, 3)),
            dma((4, 3)),
            dma((2,)),
            dma((3,)),
            dma((3,)),
        ],
        compiler_params=pltpu.CompilerParams(
            collective_id=0, has_side_effects=True, vmem_limit_bytes=40 * 1024 * 1024
        ),
        cost_estimate=pl.CostEstimate(flops=1_800_000_000, bytes_accessed=5_000_000, transcendentals=0),
    )(activations, out_grads)


def on_device(activations, out_grads, act_old, grad_old):
    total_rows = out_grads.shape[0] * lax.axis_size("dp")
    norm_scale = (1.0 - DECAY_RATE) / total_rows
    act_sum, grad_rows = statistics(activations, out_grads)
    first = (lax.axis_index("dp") % 2) * 4
    grad_sum = lax.dynamic_slice_in_dim(grad_rows, first, 4, 1)
    act_new = DECAY_RATE * act_old + norm_scale * act_sum
    grad_new = DECAY_RATE * grad_old + norm_scale * grad_sum
    return (act_new, grad_new)


def solution(mesh):
    return jax.shard_map(
        on_device,
        mesh=mesh,
        in_specs=(
            P(("dp", "tensor"), None),
            P("dp", "tensor"),
            P("tensor", "dp", None),
            P("tensor", "dp", None),
        ),
        out_specs=(P("tensor", "dp", None), P("tensor", "dp", None)),
        check_vma=False,
    )
```

```python
import functools

import jax
import jax.numpy as jnp
from jax import lax
from jax.experimental import pallas as pl
from jax.experimental.pallas import tpu as pltpu
from jax.sharding import PartitionSpec as P

MESH = pl.DeviceIdType.MESH
F32 = jnp.float32
BF16 = jnp.bfloat16
DECAY_RATE = 0.5

FIRST = BF16
X, Y, Z = 0, 1, 2
ORDERS = ((X, Y, Z), (X, Z, Y), (Y, X, Z), (Z, X, Y))


def gram(left, right):
    return lax.dot_general(left, right, (((0,), (0,)), ((), ())), preferred_element_type=F32)


def kernel(
    act_ref, grad_ref, act_out, grad_out,
    gv, xo, xc, xy, xz, xd, acc,
    a_own, a_snd, a_r1, a_s2, a_r2, a_s3, a_r3, fin, fin_r,
    g_own, g_snd, g_r1, g_s2, g_r2, g_s3, g_r3,
    local_sem, tok_send, tok_recv, a_send, a_recv, fin_sem, g_send, g_recv,
):
    dp = lax.axis_index("dp")
    tensor = lax.axis_index("tensor")
    yh = dp % 2
    x = (dp // 2) % 4
    z = dp // 8
    c = tensor % 2
    y = yh * 4 + tensor // 2
    yp, zp = y % 2, z % 2
    q, m = y // 2, z // 2

    def device(zz, xx, yy, cc):
        return ((zz * 4 + xx) * 2 + yy // 4, (yy % 4) * 2 + cc)

    def columns(half, ypar, core, zpar):
        return pl.ds(pl.multiple_of((half * 8 + ypar * 4 + core * 2 + zpar) * 512, 512), 512)

    def send(src, dst, send_sem, recv_sem, target):
        pltpu.make_async_remote_copy(
            src_ref=src, dst_ref=dst, send_sem=send_sem, recv_sem=recv_sem,
            device_id=target, device_id_type=MESH,
        ).start()

    here = (dp, tensor)

    def arrived(buf, sem):
        pltpu.make_async_remote_copy(
            src_ref=buf, dst_ref=buf, send_sem=sem, recv_sem=sem,
            device_id=here, device_id_type=MESH,
        ).wait_recv()

    def left(buf, sem):
        pltpu.make_async_remote_copy(
            src_ref=buf, dst_ref=buf, send_sem=sem, recv_sem=sem,
            device_id=here, device_id_type=MESH,
        ).wait_send()

    grads_in = pltpu.make_async_copy(grad_ref, gv, local_sem.at[0])
    grads_in.start()
    own_in = [
        pltpu.make_async_copy(act_ref.at[:, columns(h, yp, c, zp)], xo.at[h], local_sem.at[1 + h])
        for h in range(2)
    ]
    for copy in own_in:
        copy.start()

    yn = ((y + 1) % 8, (y + 7) % 8)
    zn = ((z + 1) % 8, (z + 7) % 8)
    cores = (c, 1 - c)
    oy, oz = 1 - yp, 1 - zp

    peers = [device(z, x, y, 1 - c)]
    peers += [device(z, x, yn[s], cores[f]) for s in range(2) for f in range(2)]
    peers += [device(zn[s], x, y, cores[f]) for s in range(2) for f in range(2)]
    peers += [device(zn[t], x, yn[s], cores[f]) for s in range(2) for t in range(2) for f in range(2)]
    peers += [device(z, (x + k) % 4, y, c) for k in range(1, 4)]
    peers += [device(z, x, (y + 2 * k) % 8, c) for k in range(1, 4)]
    peers += [device((z + k) % 8, x, y, c) for k in range(2, 7)]
    barrier = pltpu.get_barrier_semaphore()
    for peer in peers:
        pl.semaphore_signal(barrier, inc=1, device_id=peer, device_id_type=MESH)
    pl.semaphore_wait(barrier, len(peers))

    for s in range(2):
        for t in range(2):
            for f in range(2):
                n = s * 2 + t
                for h in range(2):
                    send(
                        act_ref.at[pl.ds(n * 32, 32), columns(h, oy, cores[f], oz)],
                        xd.at[h, pl.ds((n * 2 + f) * 32, 32)],
                        tok_send.at[3], tok_recv.at[3], device(zn[t], x, yn[s], cores[f]),
                    )
    for s in range(2):
        for f in range(2):
            for h in range(2):
                send(
                    act_ref.at[pl.ds(s * 64, 64), columns(h, oy, cores[f], zp)],
                    xy.at[h, pl.ds((s * 2 + f) * 64, 64)],
                    tok_send.at[1], tok_recv.at[1], device(z, x, yn[s], cores[f]),
                )
                send(
                    act_ref.at[pl.ds(s * 64, 64), columns(h, yp, cores[f], oz)],
                    xz.at[h, pl.ds((s * 2 + f) * 64, 64)],
                    tok_send.at[2], tok_recv.at[2], device(zn[s], x, y, cores[f]),
                )
    for h in range(2):
        send(
            act_ref.at[:, columns(h, yp, 1 - c, zp)], xc.at[h],
            tok_send.at[0], tok_recv.at[0], device(z, x, y, 1 - c),
        )

    grads_in.wait()
    for b in range(5):
        block = gv[:, b * 256:(b + 1) * 256]
        part = gram(block, block)
        for xx in range(4):
            for mm in range(4):
                r = mm * 64 + xx * 8
                rows = jnp.concatenate([part[r:r + 8], part[r + 32:r + 40]], axis=0)
                g_own[xx, mm, b] = rows
                g_snd[xx, mm, b] = rows.astype(FIRST)
    for k in range(1, 4):
        to = (x + k) % 4
        send(g_snd.at[to], g_r1.at[k - 1], g_send.at[0], g_recv.at[0], device(z, to, y, c))

    def second_gradients():
        arrived(g_r1, g_recv.at[0])
        for mm in range(4):
            for b in range(5):
                rows = g_own[x, mm, b]
                for k in range(3):
                    rows += g_r1[k, mm, b].astype(F32)
                g_s2[2 * mm, b] = rows[:8]
                g_s2[2 * mm + 1, b] = rows[8:]
        for k in (4, 3, 5, 2, 6, 1, 7):
            to = (z + k) % 8
            send(g_s2.at[to], g_r2.at[k - 1], g_send.at[1], g_recv.at[1], device(to, x, y, c))

    for copy in own_in:
        copy.wait()
    for h in range(2):
        for i in range(2):
            acc[h, i * 256:(i + 1) * 256] = gram(xo[h, :, i * 256:(i + 1) * 256], xo[h])
    for buf, g in ((xc, 0), (xy, 1), (xz, 2)):
        if g == 1:
            second_gradients()
        arrived(buf, tok_recv.at[g])
        for h in range(2):
            for i in range(2):
                acc[h, i * 256:(i + 1) * 256] += gram(buf[h, :, i * 256:(i + 1) * 256], buf[h])
    arrived(xd, tok_recv.at[3])
    for h in range(2):
        for mm in range(4):
            part = acc[h, mm * 128:(mm + 1) * 128] + gram(xd[h, :, mm * 128:(mm + 1) * 128], xd[h])
            for xx in range(4):
                for hi in range(2):
                    r = xx * 16 + hi * 8
                    rows = jnp.concatenate([part[r:r + 8], part[r + 64:r + 72]], axis=0)
                    at = (xx, hi * 2 + h, mm)
                    for p in range(4):
                        i1, i2, i3 = (at[axis] for axis in ORDERS[p])
                        piece = rows[:, p * 128:(p + 1) * 128]
                        a_own[p, i1, i2, i3] = piece
                        a_snd[p, i1, i2, i3] = piece.astype(FIRST)

    me = (x, q, m)

    def scatter(src, dst, axis, send_sem, recv_sem):
        for k in (2, 1, 3):
            to = (me[axis] + k) % 4
            target = (
                device(z, to, y, c) if axis == X
                else device(z, x, (y + 2 * k) % 8, c) if axis == Y
                else device((z + 2 * k) % 8, x, y, c)
            )
            send(src.at[to], dst.at[k - 1], send_sem, recv_sem, target)

    for p in (2, 3, 0, 1):
        scatter(a_snd.at[p], a_r1.at[p], ORDERS[p][0], a_send.at[p, 0], a_recv.at[p, 0])

    for p in range(4):
        arrived(a_r1.at[p], a_recv.at[p, 0])
        own = me[ORDERS[p][0]]
        total = a_own[p, own]
        for k in range(3):
            total += a_r1[p, k].astype(F32)
        a_s2[p] = total
        scatter(a_s2.at[p], a_r2.at[p], ORDERS[p][1], a_send.at[p, 1], a_recv.at[p, 1])

    arrived(g_r2, g_recv.at[1])
    rest = g_s2[z]
    for k in range(7):
        rest += g_r2[k]
    g_s3[...] = rest
    send(g_s3, g_r3, g_send.at[2], g_recv.at[2], device(z, x, (y + 4) % 8, c))

    for p in range(4):
        arrived(a_r2.at[p], a_recv.at[p, 1])
        own = me[ORDERS[p][1]]
        total = a_s2[p, own]
        for k in range(3):
            total += a_r2[p, k]
        a_s3[p] = total
        scatter(a_s3.at[p], a_r3.at[p], ORDERS[p][2], a_send.at[p, 2], a_recv.at[p, 2])

    for p in range(4):
        arrived(a_r3.at[p], a_recv.at[p, 2])
        own = me[ORDERS[p][2]]
        total = a_s3[p, own]
        for k in range(3):
            total += a_r3[p, k]
        fin[0, :, p * 128:(p + 1) * 128] = total[:8]
        fin[1, :, p * 128:(p + 1) * 128] = total[8:]
    partner = device(z + 1 - 2 * zp, x, y, c)
    send(fin.at[oz], fin_r, fin_sem.at[0], fin_sem.at[1], partner)
    arrived(g_r3, g_recv.at[2])
    grad_out[...] = g_s3[...] + g_r3[...]
    act_out[zp] = fin[zp]
    arrived(fin_r, fin_sem.at[1])
    act_out[oz] = fin_r[...]

    for buf, g in ((xc, 0), (xy, 1), (xz, 2), (xd, 3)):
        left(buf, tok_send.at[g])
    for p in range(4):
        left(a_r1.at[p], a_send.at[p, 0])
        left(a_r2.at[p], a_send.at[p, 1])
        left(a_r3.at[p], a_send.at[p, 2])
    left(g_r1, g_send.at[0])
    left(g_r2, g_send.at[1])
    left(g_r3, g_send.at[2])
    left(fin_r, fin_sem.at[0])


def statistics(activations, out_grads):
    any_spec = pl.BlockSpec(memory_space=pl.ANY)
    vmem_spec = pl.BlockSpec(memory_space=pltpu.VMEM)
    vmem = pltpu.VMEM
    dma = pltpu.SemaphoreType.DMA
    return pl.pallas_call(
        kernel,
        out_shape=(jax.ShapeDtypeStruct((2, 8, 512), F32), jax.ShapeDtypeStruct((5, 8, 256), F32)),
        in_specs=[any_spec, any_spec],
        out_specs=(vmem_spec, vmem_spec),
        scratch_shapes=[
            vmem((1024, 1280), BF16),
            vmem((2, 128, 512), BF16),
            vmem((2, 128, 512), BF16),
            vmem((2, 256, 512), BF16),
            vmem((2, 256, 512), BF16),
            vmem((2, 256, 512), BF16),
            vmem((2, 512, 512), F32),
            vmem((4, 4, 4, 4, 16, 128), F32),
            vmem((4, 4, 4, 4, 16, 128), FIRST),
            vmem((4, 3, 4, 4, 16, 128), FIRST),
            vmem((4, 4, 4, 16, 128), F32),
            vmem((4, 3, 4, 16, 128), F32),
            vmem((4, 4, 16, 128), F32),
            vmem((4, 3, 16, 128), F32),
            vmem((2, 8, 512), F32),
            vmem((8, 512), F32),
            vmem((4, 4, 5, 16, 256), F32),
            vmem((4, 4, 5, 16, 256), FIRST),
            vmem((3, 4, 5, 16, 256), FIRST),
            vmem((8, 5, 8, 256), F32),
            vmem((7, 5, 8, 256), F32),
            vmem((5, 8, 256), F32),
            vmem((5, 8, 256), F32),
            dma((3,)),
            dma((4,)),
            dma((4,)),
            dma((4, 3)),
            dma((4, 3)),
            dma((2,)),
            dma((3,)),
            dma((3,)),
        ],
        compiler_params=pltpu.CompilerParams(
            collective_id=0, has_side_effects=True, vmem_limit_bytes=60 * 1024 * 1024
        ),
        cost_estimate=pl.CostEstimate(flops=1_800_000_000, bytes_accessed=5_000_000, transcendentals=0),
    )(activations, out_grads)


def on_device(activations, out_grads, act_old, grad_old):
    total_rows = out_grads.shape[0] * lax.axis_size("dp")
    norm_scale = (1.0 - DECAY_RATE) / total_rows
    act_sum, grad_rows = statistics(activations, out_grads)
    first = (lax.axis_index("dp") % 2) * 4
    grad_sum = lax.dynamic_slice_in_dim(grad_rows, first, 4, 1)
    act_new = DECAY_RATE * act_old + norm_scale * act_sum
    grad_new = DECAY_RATE * grad_old + norm_scale * grad_sum
    return (act_new, grad_new)


def solution(mesh):
    return jax.shard_map(
        on_device,
        mesh=mesh,
        in_specs=(
            P(("dp", "tensor"), None),
            P("dp", "tensor"),
            P("tensor", "dp", None),
            P("tensor", "dp", None),
        ),
        out_specs=(P("tensor", "dp", None), P("tensor", "dp", None)),
        check_vma=False,
    )
```
